32 devices in a mesh: groups: 2 (over x), row: 4 (over z), col: 4 (over y, core).
Axes of the slice: x: 2, y: 2, z: 4, core: 2. Of those that a mesh axis runs over, the one named last changes fastest.
Arguments:
- probes: bfloat16 [1024, 2048], P('groups', ('row', 'col')), parts along dimension 0, may hold values from -6 to 6
- ham_blocks: bfloat16 [32, 4, 2, 128, 128], P(('groups', 'row', 'col')), parts along dimension 0, as said below
- strain_blocks: bfloat16 [32, 4, 2, 6, 128, 128], P(('groups', 'row', 'col')), parts along dimension 0, as said below
- block_cols: int32 [32, 4, 2], P(('groups', 'row', 'col')), parts along dimension 0, may hold values from -1 to 15, as said below
- odd_coeffs: float32 [2], replicated, may hold values from 0.5 to 1.5
Outputs:
- density: bfloat16 [1024, 2048], P('groups', ('col', 'row')), parts along dimension 0
- stress: float32 [12, 16], P('groups', 'row'), parts along dimension 0
The draws below stay inside these ranges and needn't reach their ends.
There are 2 independent parts, one for each index of `groups`. The reference program is written for one: setup_inputs(seed, part) draws one part's arguments, and reference() takes and returns one part's arrays. A program takes and returns all parts, laid end to end along the dimension named above; an argument that names none is the same for every part. Nothing has to cross between parts.
Inputs may be any that keep to these rules, and one draw needn't show every extreme that they name: block_cols[i,g,s] is -1 or a block column of group g (from g * 4 to g * 4 + 3); the filled slots of a group come first and name distinct columns; every block row has exactly 2 filled slots in its own group (the one holding column i); the pattern is symmetric: column j is named in row i exactly when column i is named in row j. `ham_blocks`: the slot of an empty block_cols entry holds zeros; block (j, i) is the transpose of block (i, j), so H is symmetric. `strain_blocks`: the slot of an empty block_cols entry holds zeros; block (j, i) is the transpose of block (i, j) in every component.
All inputs are finite; a program needn't handle non-finite values.
Results may differ from the reference program's by a relative error of at most 0.023.
Values may be sent and summed in bfloat16 or wider, within the bound.
A program may use at most 128 MiB of HBM per device.

```python
import math
import jax
import jax.numpy as jnp
from jax import lax

BLK = 128
P_SIZE = 512
CAP = 2
COMP = 6
RB = 4
CB = 4
NB = 16
NG = 4
N = 2048
N_ROW = 4


def block_pattern(key):
    row_ids = jnp.arange(NB, dtype=jnp.int32)
    group_ids = jnp.arange(NG, dtype=jnp.int32)
    slot_ids = jnp.arange(CAP, dtype=jnp.int32)

    def one_entry(row_id, group_id):
        own_group = row_id // CB
        within = row_id % CB
        lower = jnp.minimum(own_group, group_id)
        higher = jnp.maximum(own_group, group_id)
        pair_key = jax.random.fold_in(key, lower * NG + higher)
        ordering = jax.random.permutation(jax.random.fold_in(pair_key, 1), CB).astype(jnp.int32)
        inverse = jnp.argsort(ordering).astype(jnp.int32)
        drawn_count = jax.random.randint(jax.random.fold_in(pair_key, 2), (), 0, CAP + 1)
        filled_count = jnp.where(own_group == group_id, CAP, drawn_count)
        offset = jax.random.randint(jax.random.fold_in(pair_key, 3), (), 0, CB)
        upward = (ordering[within] + offset + slot_ids) % CB
        downward = inverse[(within - offset - slot_ids) % CB]
        inside = inverse[(offset + slot_ids - ordering[within]) % CB]
        target = jnp.where(own_group < group_id, upward, jnp.where(own_group > group_id, downward, inside))
        return jnp.where(slot_ids < filled_count, group_id * CB + target, -1).astype(jnp.int32)

    def one_row(row_id):
        return jax.vmap(lambda group_id: one_entry(row_id, group_id))(group_ids)
    return jax.vmap(one_row)(row_ids)


def block_values(key, columns_all, depth, scale):

    def one_row(row_id):

        def one_slot(column):
            lower = jnp.maximum(jnp.minimum(row_id, column), 0)
            higher = jnp.maximum(row_id, column)
            slot_key = jax.random.fold_in(key, lower * NB + higher)
            normal_part = jax.random.normal(jax.random.fold_in(slot_key, 1), (depth, BLK, BLK), jnp.float32)
            mixed = normal_part
            flipped = jnp.swapaxes(mixed, 1, 2)
            chosen = jnp.where(row_id < column, mixed, jnp.where(row_id > column, flipped, (mixed + flipped) * 0.70710678))
            return jnp.where(column >= 0, chosen * scale, 0.0)
        return jax.vmap(jax.vmap(one_slot))(columns_all[row_id])
    return lax.map(one_row, jnp.arange(NB, dtype=jnp.int32))


def draw_block_cols(key, part):
    return block_pattern(key)


def draw_ham_blocks(key, part):
    columns_all = block_pattern(key)
    key = jax.random.fold_in(key, 17)
    mean_filled = CAP + (NG - 1) * CAP / 2.0
    values = block_values(key, columns_all, 1, 0.45 / math.sqrt(BLK * mean_filled))
    return values.reshape(NB, NG, CAP, BLK, BLK).astype(jnp.bfloat16)


def draw_strain_blocks(key, part):
    columns_all = block_pattern(key)
    key = jax.random.fold_in(key, 29)
    mean_filled = CAP + (NG - 1) * CAP / 2.0
    return block_values(key, columns_all, COMP, math.sqrt(P_SIZE) / (BLK * math.sqrt(mean_filled))).astype(jnp.bfloat16)


def levels(stream_key, extent, split, least, largest):
    loudness, own = 1.0, jax.random.fold_in(stream_key, 6)
    for dim, shards_of in split:
        heights = jnp.exp(jax.random.uniform(jax.random.fold_in(own, dim), (shards_of,), jnp.float32, least / len(split), largest / len(split)))
        loudness = loudness * jnp.repeat(heights, extent[dim] // shards_of).reshape([-1 if axis == dim else 1 for axis in range(len(extent))])
    return loudness


def centred(key, shape, spread, most, shards=(), kind=jnp.bfloat16):
    loudness = levels(key, shape, shards, -0.22, 0.18) if shards else 1.0
    values = jax.random.normal(key, shape, jnp.float32) * spread * loudness
    return jnp.minimum(jnp.maximum(values, -most), most).astype(kind)


def setup_inputs(seed: int = 0, part: int = 0) -> dict:
    splits = jax.random.split(jax.random.key(seed), 6)
    part_splits = jax.random.split(jax.random.fold_in(splits[5], part), 6)
    return {
        "probes": centred(part_splits[0], (P_SIZE, N), 1.0, 6.0, ((1, 16),)),
        "ham_blocks": draw_ham_blocks(jax.random.fold_in(jax.random.fold_in(splits[5], part), 71), part),
        "strain_blocks": draw_strain_blocks(jax.random.fold_in(jax.random.fold_in(splits[5], part), 71), part),
        "block_cols": draw_block_cols(jax.random.fold_in(jax.random.fold_in(splits[5], part), 71), part),
        "odd_coeffs": jnp.clip(jax.random.uniform(splits[4], (2,), jnp.float32, 0.5, 1.5), 0.5, 1.5),
    }


def grouped_product(panel, ham_rows, col_rows, group_count, group_span):
    probe_count = panel.shape[0]
    block_size = ham_rows.shape[-1]
    blocks_total = ham_rows.shape[0]
    panel_blocks = panel.reshape(probe_count, blocks_total, block_size)

    def one_row(row_index):
        columns = col_rows[row_index]
        safe_cols = jnp.clip(columns, 0, blocks_total - 1).astype(jnp.int32)
        picked = jnp.take(panel_blocks, safe_cols, axis=1).astype(jnp.float32)
        blocks = ham_rows[row_index].astype(jnp.float32)
        contrib = jnp.einsum("psb,sab->spa", picked, blocks)
        groups = (safe_cols // group_span).astype(jnp.int32)
        onehot = (groups[:, None] == jnp.arange(group_count, dtype=jnp.int32)[None, :]).astype(jnp.float32)
        partial_value = jnp.einsum("spa,sg->gpa", contrib, onehot, precision=lax.Precision.HIGHEST)
        rounded = lax.optimization_barrier(partial_value.astype(jnp.bfloat16)).astype(jnp.float32)
        return jnp.sum(rounded, axis=0)

    result_rows = lax.map(one_row, jnp.arange(blocks_total, dtype=jnp.int32))
    return jnp.transpose(result_rows, (1, 0, 2)).reshape(probe_count, blocks_total * block_size)


def reference(probes, ham_blocks, strain_blocks, block_cols, odd_coeffs):
    ham_rows = ham_blocks.reshape(NB, NG * CAP, BLK, BLK)
    strain_rows = strain_blocks.reshape(NB, NG * CAP, COMP, BLK, BLK)
    col_rows = block_cols.reshape(NB, NG * CAP)
    first_term = grouped_product(probes, ham_rows, col_rows, N_ROW, RB).astype(jnp.bfloat16)
    second_sum = grouped_product(first_term, ham_rows, col_rows, NG, CB)
    second_term = (2.0 * second_sum - probes.astype(jnp.float32)).astype(jnp.bfloat16)
    third_sum = grouped_product(second_term, ham_rows, col_rows, N_ROW, RB)
    third_term = 2.0 * third_sum - first_term.astype(jnp.float32)
    density = (odd_coeffs[0] * first_term.astype(jnp.float32) + odd_coeffs[1] * third_term).astype(jnp.bfloat16)
    density_blocks = density.reshape(P_SIZE, NB, BLK)

    def row_stress(row_index):
        columns = col_rows[row_index]
        safe_cols = jnp.clip(columns, 0, NB - 1).astype(jnp.int32)
        start = (row_index * BLK).astype(jnp.int32)
        own_part = lax.dynamic_slice_in_dim(probes, start, BLK, 1).astype(jnp.float32)
        others = jnp.take(density_blocks, safe_cols, axis=1).astype(jnp.float32)
        pair_tiles = jnp.einsum("pa,psb->sab", own_part, others)
        pair_tiles = lax.optimization_barrier(pair_tiles.astype(jnp.bfloat16)).astype(jnp.float32)
        return jnp.einsum("skab,sab->k", strain_rows[row_index].astype(jnp.float32), pair_tiles) / P_SIZE

    stress = lax.map(row_stress, jnp.arange(NB, dtype=jnp.int32))
    return density, jnp.transpose(stress, (1, 0))
```

```python
import functools

import jax
import jax.numpy as jnp
from jax import lax
from jax.experimental import pallas as pl
from jax.experimental.pallas import tpu as pltpu
from jax.sharding import PartitionSpec as P

MESH = pl.DeviceIdType.MESH


def fused_kernel(
    n_row,
    probes_ref, ham_ref, strain_ref, cols_ref, coeffs_ref,
    out_ref, stress_ref,
    hbuf, pbuf, xbuf, cbuf, csm, sbuf, strain_buf, x0t, x1t, x2t, dsend, dmine,
    hs, hr, ps, pr, xs, xr, cs, cr, das, dar, dbs, dbr, ss, sr, loc,
):
    n_col = 4
    nb = n_row * n_col
    grp = lax.axis_index("groups")
    z = lax.axis_index("row")
    c = lax.axis_index("col")
    me = z * n_col + c
    sib = c + 1 - 2 * (c % 2)
    yc = (c + 2) % 4
    ysib = sib + 2 - 4 * (sib // 2)
    slots = hbuf.shape[1]
    chunks = hr.shape[1]
    per = slots // chunks
    sub = xbuf.shape[1]
    comps = strain_buf.shape[1]

    def dev(row, col):
        return (grp, row, col)

    def others():
        for d in range(1, nb):
            k = (me + d) % nb
            yield d, k

    barrier = pltpu.get_barrier_semaphore()
    for _, k in others():
        pl.semaphore_signal(barrier, inc=1, device_id=dev(k // n_col, k % n_col), device_id_type=MESH)
    strain_copy = pltpu.make_async_copy(strain_ref, strain_buf, loc.at[0])
    strain_copy.start()
    own_ham = pltpu.make_async_copy(ham_ref, hbuf.at[me], loc.at[1])
    own_ham.start()
    pbuf[me] = probes_ref[...]
    cbuf[me] = cols_ref[...]
    xbuf[me] = probes_ref[pl.ds(pl.multiple_of(me * sub, sub), sub), :]
    pl.semaphore_wait(barrier, nb - 1)

    waits = []

    def remote(src, dst, send, recv, target):
        return pltpu.make_async_remote_copy(
            src_ref=src, dst_ref=dst, send_sem=send, recv_sem=recv, device_id=target, device_id_type=MESH
        )

    def launch(copy, pred=None):
        if pred is None:
            copy.start()
        else:
            @pl.when(pred)
            def _():
                copy.start()
        waits.append((copy, pred))

    def small(src_of, dst, send, recv, place=lambda k: (k // n_col, k % n_col)):
        for d, k in others():
            launch(remote(src_of(k), dst, send.at[d], recv.at[me], dev(*place(k))))

    def small_wait(dst, send, recv):
        for d, k in others():
            remote(dst.at[k], dst.at[k], send.at[d], recv.at[k], dev(z, sib)).wait_recv()

    small(lambda k: cbuf.at[me], cbuf.at[me], cs, cr)
    small(lambda k: probes_ref.at[pl.ds(pl.multiple_of(k * sub, sub), sub)], xbuf.at[me], xs, xr)

    def ham_piece(org, m):
        return hbuf.at[org, pl.ds(m * per, per)]

    def ham_send(org, m, way, target, pred=None):
        src = ham_ref.at[pl.ds(m * per, per)] if org is me else ham_piece(org, m)
        launch(remote(src, ham_piece(org, m), hs.at[org, m, way], hr.at[org, m], target), pred)

    def ham_recv(org, m):
        remote(ham_piece(org, m), ham_piece(org, m), hs.at[org, m, 0], hr.at[org, m], dev(z, sib)).wait_recv()

    def probe_send(org, m, way, target, pred=None):
        launch(remote(pbuf.at[org], pbuf.at[org], ps.at[org, way], pr.at[org], target), pred)

    def probe_recv(org, m):
        remote(pbuf.at[org], pbuf.at[org], ps.at[org, 0], pr.at[org], dev(z, sib)).wait_recv()

    up, down = z + 1, z - 1
    has_up, has_down = z < n_row - 1, z > 0

    def first(send, pieces):
        for m in range(pieces):
            send(me, m, 0, dev(jnp.minimum(up, n_row - 1), c), has_up)
            send(me, m, 1, dev(jnp.maximum(down, 0), c), has_down)
            send(me, m, 2, dev(z, yc))
            send(me, m, 3, dev(z, sib))

    def wave(d, send, recv, pieces):
        for m in range(pieces):
            if d < n_row:
                for sgn in (-1, 1):
                    zo = z + sgn * d
                    ok = zo >= 0 if sgn < 0 else zo <= n_row - 1
                    org = jnp.clip(zo, 0, n_row - 1) * n_col + c

                    @pl.when(ok)
                    def _():
                        recv(org, m)
                    if d < n_row - 1:
                        if sgn < 0:
                            send(org, m, 0, dev(jnp.minimum(up, n_row - 1), c), jnp.logical_and(ok, has_up))
                        else:
                            send(org, m, 1, dev(jnp.maximum(down, 0), c), jnp.logical_and(ok, has_down))
                    send(org, m, 2, dev(z, yc), ok)
                    send(org, m, 3, dev(z, sib), ok)
            for sgn in (-1, 1) if d > 1 else (1,):
                zo = z + sgn * (d - 1)
                ok = zo >= 0 if sgn < 0 else zo <= n_row - 1
                org = jnp.clip(zo, 0, n_row - 1) * n_col + yc

                @pl.when(ok)
                def _():
                    recv(org, m)
                send(org, m, 3, dev(z, sib), ok)

    def last(recv, pieces):
        for row in range(n_row):
            for m in range(pieces):
                recv(row * n_col + sib, m)
                recv(row * n_col + ysib, m)

    first(ham_send, chunks)
    first(probe_send, 1)

    small_wait(cbuf, cs, cr)
    cols_copy = pltpu.make_async_copy(cbuf, csm, loc.at[2])
    cols_copy.start()
    small_wait(xbuf, xs, xr)
    for j in range(nb):
        x0t[j] = xbuf[j].astype(jnp.float32).T.astype(jnp.bfloat16)
    cols_copy.wait()

    for d in range(1, n_row + 1):
        wave(d, ham_send, ham_recv, chunks)
    own_ham.wait()
    last(ham_recv, chunks)

    groups = csm.shape[1]
    cap = csm.shape[2]

    def col_of(i, s):
        return jnp.clip(csm[i, s // cap, s % cap], 0, nb - 1)

    def product(x_ref, i):
        weights = jnp.concatenate([x_ref[col_of(i, s)] for s in range(slots)], axis=0)
        rows = jnp.concatenate([hbuf[i, s] for s in range(slots)], axis=1)
        return jnp.dot(rows, weights, preferred_element_type=jnp.float32)

    def one(i, carry):
        x1t[i] = product(x0t, i).astype(jnp.bfloat16)
        return carry

    def two(i, carry):
        x2t[i] = (2.0 * product(x1t, i) - x0t[i].astype(jnp.float32)).astype(jnp.bfloat16)
        return carry

    def three(i, carry):
        prior = x1t[i].astype(jnp.float32)
        third = 2.0 * product(x2t, i) - prior
        dense = coeffs_ref[0] * prior + coeffs_ref[1] * third
        dsend[i] = dense.T.astype(jnp.bfloat16)
        return carry

    wave(1, probe_send, probe_recv, 1)
    lax.fori_loop(0, nb, one, 0)
    wave(2, probe_send, probe_recv, 1)
    lax.fori_loop(0, nb, two, 0)
    wave(3, probe_send, probe_recv, 1)
    lax.fori_loop(0, nb, three, 0)

    small(lambda k: dsend.at[k], dmine.at[me], das, dar)
    dmine[me] = dsend[me]

    def swap(k):
        return (k % n_col, k // n_col)

    mine_out = c * n_row + z
    for d in range(1, nb):
        k = (mine_out + d) % nb
        row, col = k % n_row, k // n_row
        launch(remote(dsend.at[k], out_ref.at[me], dbs.at[d], dbr.at[me], dev(row, col)))
    out_ref[me] = dsend[mine_out]
    for d in range(4, n_row + 1):
        wave(d, probe_send, probe_recv, 1)
    last(probe_recv, 1)

    small_wait(dmine, das, dar)
    strain_copy.wait()
    dens = dmine[...].reshape(nb * sub, dmine.shape[2])
    dens_t = dens.astype(jnp.float32).T.astype(jnp.bfloat16)
    lane = lax.broadcasted_iota(jnp.int32, (comps, 128), 1)
    part = jnp.zeros((comps, 128), jnp.float32)
    for s in range(slots):
        col = col_of(me, s)
        tile = jnp.dot(dens_t, pbuf[col], preferred_element_type=jnp.float32)
        sums = jnp.concatenate(
            [
                jnp.sum(strain_buf[s, k].astype(jnp.float32) * tile, axis=0, keepdims=True)
                for k in range(comps)
            ],
            axis=0,
        )
        part = part + jnp.where(lane == col, jnp.sum(sums, axis=1, keepdims=True), 0.0)
    sbuf[me] = jnp.concatenate([part, jnp.zeros((sbuf.shape[1] - comps, 128), jnp.float32)], axis=0)
    small(lambda k: sbuf.at[me], sbuf.at[me], ss, sr)
    small_wait(out_ref, dbs, dbr)
    small_wait(sbuf, ss, sr)
    total = jnp.sum(sbuf[...], axis=0) * (1.0 / (nb * sub))
    picked = total[:comps, 0:n_col]
    for row in range(1, n_row):
        picked = jnp.where(z == row, total[:comps, row * n_col:(row + 1) * n_col], picked)
    stress_ref[...] = picked

    for copy, pred in waits:
        if pred is None:
            copy.wait_send()
        else:
            @pl.when(pred)
            def _(copy=copy):
                copy.wait_send()


def fused_local(n_row, probes, ham_blocks, strain_blocks, block_cols, odd_coeffs):
    n_col = 4
    nb = n_row * n_col
    probe_count, block = probes.shape
    _, groups, cap, comps = strain_blocks.shape[:4]
    slots = groups * cap
    sub = probe_count // nb
    chunks = 2
    bf16, f32 = jnp.bfloat16, jnp.float32
    dma = pltpu.SemaphoreType.DMA
    vmem = pl.BlockSpec(memory_space=pltpu.VMEM)
    hbm = pl.BlockSpec(memory_space=pl.ANY)
    density, stress = pl.pallas_call(
        functools.partial(fused_kernel, n_row),
        out_shape=(
            jax.ShapeDtypeStruct((nb, sub, block), bf16),
            jax.ShapeDtypeStruct((comps, n_col), f32),
        ),
        in_specs=[vmem, hbm, hbm, vmem, pl.BlockSpec(memory_space=pltpu.SMEM)],
        out_specs=(vmem, vmem),
        scratch_shapes=[
            pltpu.VMEM((nb, slots, block, block), bf16),
            pltpu.VMEM((nb, probe_count, block), bf16),
            pltpu.VMEM((nb, sub, block), bf16),
            pltpu.VMEM((nb, groups, cap), jnp.int32),
            pltpu.SMEM((nb, groups, cap), jnp.int32),
            pltpu.VMEM((nb, 8, 128), f32),
            pltpu.VMEM((slots, comps, block, block), bf16),
            pltpu.VMEM((nb, block, sub), bf16),
            pltpu.VMEM((nb, block, sub), bf16),
            pltpu.VMEM((nb, block, sub), bf16),
            pltpu.VMEM((nb, sub, block), bf16),
            pltpu.VMEM((nb, sub, block), bf16),
            dma((nb, chunks, 4)), dma((nb, chunks)),
            dma((nb, 4)), dma((nb,)),
            dma((nb,)), dma((nb,)),
            dma((nb,)), dma((nb,)),
            dma((nb,)), dma((nb,)),
            dma((nb,)), dma((nb,)),
            dma((nb,)), dma((nb,)),
            dma((3,)),
        ],
        compiler_params=pltpu.CompilerParams(
            collective_id=0, has_side_effects=True, vmem_limit_bytes=40 * 1024 * 1024
        ),
    )(
        probes,
        ham_blocks.reshape(slots, block, block),
        strain_blocks.reshape(slots, comps, block, block),
        block_cols.reshape(groups, cap),
        odd_coeffs,
    )
    return density.reshape(probe_count, block), stress


def along_row(panel):
    return lax.all_gather(panel, "col", axis=1, tiled=True)


def along_col(panel):
    return lax.all_gather(panel, "row", axis=1, tiled=True)


def down_sum(partial_value):
    return lax.psum_scatter(
        partial_value.astype(jnp.bfloat16), "row", scatter_dimension=1, tiled=True
    ).astype(jnp.float32)


def local(probes, ham_blocks, strain_blocks, block_cols, odd_coeffs):
    probe_count = probes.shape[0]
    block_size = ham_blocks.shape[-1]
    own_rows = probes.shape[1] // block_size
    components = strain_blocks.shape[3]
    ham_local, strain_local, cols_local = (
        lax.all_to_all(ham_blocks, "col", split_axis=1, concat_axis=0, tiled=True),
        lax.all_to_all(strain_blocks, "col", split_axis=1, concat_axis=0, tiled=True),
        lax.all_to_all(block_cols, "col", split_axis=1, concat_axis=0, tiled=True),
    )
    grid_rows = ham_local.shape[0]
    slot_cap = ham_local.shape[2]
    slot_count = grid_rows * slot_cap
    ham_slots = ham_local.reshape(slot_count, block_size, block_size)
    col_slots = cols_local.reshape(slot_count)
    group_width = lax.axis_size("row") * own_rows
    local_cols = col_slots - lax.axis_index("col") * group_width
    filled = col_slots >= 0
    safe_cols = jnp.clip(local_cols, 0, group_width - 1).astype(jnp.int32)
    placement = (
        (safe_cols[:, None] == jnp.arange(group_width, dtype=jnp.int32)[None, :]) & filled[:, None]
    ).astype(jnp.float32)

    def backward(gathered):
        spread = jnp.repeat(gathered.reshape(probe_count, grid_rows, block_size), slot_cap, axis=1)
        contrib = jnp.einsum("psa,sab->psb", spread, ham_slots, preferred_element_type=jnp.float32)
        placed = jnp.einsum("psb,sj->pjb", contrib, placement, precision=lax.Precision.HIGHEST)
        return placed.reshape(probe_count, group_width * block_size)

    probes_row = along_row(probes)
    first_term = down_sum(backward(probes_row)).astype(jnp.bfloat16)
    first_col = along_col(first_term)
    picked = jnp.take(first_col.reshape(probe_count, group_width, block_size), safe_cols, axis=1)
    contrib = jnp.einsum("psb,sab->psa", picked, ham_slots, preferred_element_type=jnp.float32)
    summed = contrib.reshape(probe_count, grid_rows, slot_cap, block_size).sum(axis=2)
    partial_two = summed.reshape(probe_count, grid_rows * block_size)
    row_piece = lax.psum_scatter(
        partial_two.astype(jnp.bfloat16), "col", scatter_dimension=1, tiled=True
    ).astype(jnp.float32)
    second_term = (2.0 * row_piece - probes.astype(jnp.float32)).astype(jnp.bfloat16)
    second_row = along_row(second_term)
    third_term = 2.0 * down_sum(backward(second_row)) - first_term.astype(jnp.float32)
    density = (odd_coeffs[0] * first_term.astype(jnp.float32) + odd_coeffs[1] * third_term).astype(
        jnp.bfloat16
    )
    density_col = along_col(density)
    own_probes = jnp.repeat(
        probes_row.reshape(probe_count, grid_rows, block_size), slot_cap, axis=1
    )
    others = jnp.take(density_col.reshape(probe_count, group_width, block_size), safe_cols, axis=1)
    pair_tiles = jnp.einsum(
        "psa,psb->sab", own_probes, others, preferred_element_type=jnp.float32
    ).astype(jnp.bfloat16)
    strain_slots = strain_local.reshape(slot_count, components, block_size, block_size)
    slot_terms = jnp.einsum(
        "skab,sab->ks", strain_slots, pair_tiles, preferred_element_type=jnp.float32
    )
    row_terms = slot_terms.reshape(components, grid_rows, slot_cap).sum(axis=2) / probe_count
    stress = lax.psum(row_terms, "col")
    return (density, stress)


def solution(mesh):
    placed = (
        P("groups", ("row", "col")),
        P(("groups", "row", "col"), None, None, None, None),
        P(("groups", "row", "col"), None, None, None, None, None),
        P(("groups", "row", "col"), None, None),
        P(),
    )
    n_row, n_col = mesh.shape["row"], mesh.shape["col"]

    def pick(*args):
        probes, ham_blocks = args[0], args[1]
        one_block = probes.shape[1] == ham_blocks.shape[-1] and ham_blocks.shape[0] == 1
        held = n_row * n_col * (2 * ham_blocks.size + 2 * probes.size)
        whole_rows = probes.shape[0] % (16 * n_row * n_col) == 0
        if n_row == 4 and n_col == 4 and one_block and whole_rows and held <= 16 * 1024 * 1024:
            return fused_local(n_row, *args)
        return local(*args)

    return jax.shard_map(
        pick,
        mesh=mesh,
        in_specs=placed,
        out_specs=(P("groups", ("col", "row")), P("groups", "row")),
        check_vma=False,
    )
```

```python
import functools

import jax
import jax.numpy as jnp
from jax import lax
from jax.experimental import pallas as pl
from jax.experimental.pallas import tpu as pltpu
from jax.sharding import PartitionSpec as P

MESH = pl.DeviceIdType.MESH


def fused_kernel(
    n_row,
    probes_ref, ham_ref, strain_ref, cols_ref, coeffs_ref,
    out_ref, stress_ref,
    hbuf, pbuf, xbuf, cbuf, csm, coeffs, sbuf, strain_buf, x0t, x1t, x2t, dsend, dmine,
    hs, hr, ps, pr, xs, xr, cs, cr, das, dar, dbs, dbr, ss, sr, loc,
):
    n_col = 4
    nb = n_row * n_col
    grp = lax.axis_index("groups")
    z = lax.axis_index("row")
    c = lax.axis_index("col")
    me = z * n_col + c
    sib = c + 1 - 2 * (c % 2)
    yc = (c + 2) % 4
    ysib = sib + 2 - 4 * (sib // 2)
    groups, cap = hbuf.shape[1:3]
    slots = groups * cap
    chunks = hr.shape[1]
    sub = xbuf.shape[1]
    comps = strain_buf.shape[1]

    def dev(row, col):
        return (grp, row, col)

    def others():
        for d in range(1, nb):
            k = (me + d) % nb
            yield d, k

    barrier = pltpu.get_barrier_semaphore()
    for _, k in others():
        pl.semaphore_signal(barrier, inc=1, device_id=dev(k // n_col, k % n_col), device_id_type=MESH)
    own = pl.ds(pl.multiple_of(me * sub, sub), sub)
    local_copies = [
        pltpu.make_async_copy(src, dst, loc.at[n])
        for n, (src, dst) in enumerate(
            [
                (cols_ref, cbuf.at[me]),
                (probes_ref.at[own], xbuf.at[me]),
                (coeffs_ref, coeffs),
                (ham_ref, hbuf.at[me]),
                (probes_ref, pbuf.at[me]),
                (strain_ref, strain_buf),
            ]
        )
    ]
    for copy in local_copies:
        copy.start()
    pl.semaphore_wait(barrier, nb - 1)

    waits = []

    def remote(src, dst, send, recv, target):
        return pltpu.make_async_remote_copy(
            src_ref=src, dst_ref=dst, send_sem=send, recv_sem=recv, device_id=target, device_id_type=MESH
        )

    def launch(copy, pred=None):
        if pred is None:
            copy.start()
        else:
            @pl.when(pred)
            def _():
                copy.start()
        waits.append((copy, pred))

    def small(src_of, dst, send, recv, place=lambda k: (k // n_col, k % n_col)):
        for d, k in others():
            launch(remote(src_of(k), dst, send.at[d], recv.at[me], dev(*place(k))))

    def small_wait(dst, send, recv):
        for d, k in others():
            remote(dst.at[k], dst.at[k], send.at[d], recv.at[k], dev(z, sib)).wait_recv()

    small(lambda k: cols_ref, cbuf.at[me], cs, cr)
    small(lambda k: probes_ref.at[pl.ds(pl.multiple_of(k * sub, sub), sub)], xbuf.at[me], xs, xr)

    def sends_third(row):
        return jnp.logical_or(row == 0, row == n_row - 1)

    def ham_piece(org, m):
        return hbuf.at[org, (org // n_col + m) % groups]

    def with_third(org, m, pred):
        if m < 2:
            return pred
        third = sends_third(org // n_col)
        return third if pred is None else jnp.logical_and(pred, third)

    def ham_send(org, m, way, target, pred=None):
        src = ham_ref.at[(z + m) % groups] if org is me else ham_piece(org, m)
        launch(
            remote(src, ham_piece(org, m), hs.at[org, m, way], hr.at[org, m], target),
            with_third(org, m, pred),
        )

    def ham_recv(org, m):
        copy = remote(ham_piece(org, m), ham_piece(org, m), hs.at[org, m, 0], hr.at[org, m], dev(z, sib))
        if m < 2:
            copy.wait_recv()
        else:
            @pl.when(sends_third(org // n_col))
            def _():
                copy.wait_recv()

    def probe_send(org, m, way, target, pred=None):
        src = probes_ref if org is me else pbuf.at[org]
        launch(remote(src, pbuf.at[org], ps.at[org, way], pr.at[org], target), pred)

    def probe_recv(org, m):
        remote(pbuf.at[org], pbuf.at[org], ps.at[org, 0], pr.at[org], dev(z, sib)).wait_recv()

    up, down = z + 1, z - 1
    has_up, has_down = z < n_row - 1, z > 0

    def first(send, pieces):
        for m in range(pieces):
            send(me, m, 0, dev(jnp.minimum(up, n_row - 1), c), has_up)
            send(me, m, 1, dev(jnp.maximum(down, 0), c), has_down)
            send(me, m, 2, dev(z, yc))
            send(me, m, 3, dev(z, sib))

    def wave(d, send, recv, pieces):
        for m in range(pieces):
            if d < n_row:
                for sgn in (-1, 1):
                    zo = z + sgn * d
                    ok = zo >= 0 if sgn < 0 else zo <= n_row - 1
                    org = jnp.clip(zo, 0, n_row - 1) * n_col + c

                    @pl.when(ok)
                    def _():
                        recv(org, m)
                    if d < n_row - 1:
                        if sgn < 0:
                            send(org, m, 0, dev(jnp.minimum(up, n_row - 1), c), jnp.logical_and(ok, has_up))
                        else:
                            send(org, m, 1, dev(jnp.maximum(down, 0), c), jnp.logical_and(ok, has_down))
                    send(org, m, 2, dev(z, yc), ok)
                    send(org, m, 3, dev(z, sib), ok)
            for sgn in (-1, 1) if d > 1 else (1,):
                zo = z + sgn * (d - 1)
                ok = zo >= 0 if sgn < 0 else zo <= n_row - 1
                org = jnp.clip(zo, 0, n_row - 1) * n_col + yc

                @pl.when(ok)
                def _():
                    recv(org, m)
                send(org, m, 3, dev(z, sib), ok)

    def last(recv, pieces):
        for row in range(n_row):
            for m in range(pieces):
                recv(row * n_col + sib, m)
                recv(row * n_col + ysib, m)

    first(ham_send, chunks)
    first(probe_send, 1)

    small_wait(cbuf, cs, cr)
    local_copies[0].wait()
    cols_copy = pltpu.make_async_copy(cbuf, csm, loc.at[6])
    cols_copy.start()
    small_wait(xbuf, xs, xr)
    local_copies[1].wait()
    for j in range(nb):
        x0t[j] = xbuf[j].astype(jnp.float32).T.astype(jnp.bfloat16)
    cols_copy.wait()
    local_copies[2].wait()

    for d in range(1, n_row + 1):
        wave(d, ham_send, ham_recv, chunks)
    local_copies[3].wait()
    last(ham_recv, chunks)

    wave(1, probe_send, probe_recv, 1)

    def col_of(i, s):
        return jnp.clip(csm[i, s % cap, s // cap], 0, nb - 1)

    def mirror(a, g):
        def one_row(w, carry):
            i = a * n_col + w
            for s in range(cap):
                raw = csm[i, s, g]
                j = jnp.clip(raw, 0, nb - 1)
                place = jnp.int32(0)
                for t in range(1, cap):
                    place = jnp.where(csm[j, t, a] == i, t, place)
                block = hbuf[j, a, place].T
                hbuf[i, g, s] = jnp.where(raw >= 0, block, jnp.zeros_like(block))
            return carry

        lax.fori_loop(0, n_col, one_row, 0, unroll=True)

    for g in range(groups):
        mirror((g + 1) % groups, g)
        if g in (0, n_row - 1):
            mirror((g + 2) % groups, g)

    def product(x_ref, i):
        weights = jnp.concatenate([x_ref[col_of(i, s)] for s in range(slots)], axis=0)
        rows = jnp.concatenate([hbuf[i, s // cap, s % cap] for s in range(slots)], axis=1)
        return jnp.dot(rows, weights, preferred_element_type=jnp.float32)

    def one(i, carry):
        x1t[i] = product(x0t, i).astype(jnp.bfloat16)
        return carry

    def two(i, carry):
        x2t[i] = (2.0 * product(x1t, i) - x0t[i].astype(jnp.float32)).astype(jnp.bfloat16)
        return carry

    mine_out = c * n_row + z

    def density_copies(k):
        return (
            (k != me, remote(dsend.at[k], dmine.at[me], das.at[k], dar.at[me], dev(k // n_col, k % n_col))),
            (k != mine_out, remote(dsend.at[k], out_ref.at[me], dbs.at[k], dbr.at[me], dev(k % n_row, k // n_row))),
        )

    def three(t, carry):
        i = (me + 1 + t) % nb
        prior = x1t[i].astype(jnp.float32)
        third = 2.0 * product(x2t, i) - prior
        dense = coeffs[0] * prior + coeffs[1] * third
        dsend[i] = dense.T.astype(jnp.bfloat16)
        for pred, copy in density_copies(i):
            pl.when(pred)(copy.start)
        return carry

    lax.fori_loop(0, nb, one, 0, unroll=2)
    wave(2, probe_send, probe_recv, 1)
    lax.fori_loop(0, nb, two, 0, unroll=2)
    wave(3, probe_send, probe_recv, 1)
    lax.fori_loop(0, nb, three, 0)
    dmine[me] = dsend[me]
    out_ref[me] = dsend[mine_out]
    for d in range(4, n_row + 1):
        wave(d, probe_send, probe_recv, 1)
    last(probe_recv, 1)

    small_wait(dmine, das, dar)
    local_copies[4].wait()
    local_copies[5].wait()
    dens = dmine[...].reshape(nb * sub, dmine.shape[2])
    dens_t = dens.astype(jnp.float32).T.astype(jnp.bfloat16)
    lane = lax.broadcasted_iota(jnp.int32, (comps, 128), 1)
    part = jnp.zeros((comps, 128), jnp.float32)
    for s in range(slots):
        col = col_of(me, s)
        tile = jnp.dot(dens_t, pbuf[col], preferred_element_type=jnp.float32)
        sums = jnp.concatenate(
            [
                jnp.sum(strain_buf[s, k].astype(jnp.float32) * tile, axis=0, keepdims=True)
                for k in range(comps)
            ],
            axis=0,
        )
        part = part + jnp.where(lane == col, jnp.sum(sums, axis=1, keepdims=True), 0.0)
    sbuf[me] = jnp.concatenate([part, jnp.zeros((sbuf.shape[1] - comps, 128), jnp.float32)], axis=0)
    small(lambda k: sbuf.at[me], sbuf.at[me], ss, sr)
    for k in range(nb):
        for pred, copy in density_copies(k):
            pl.when(pred)(copy.wait_send)
    for copy, pred in waits:
        if pred is None:
            copy.wait_send()
        else:
            @pl.when(pred)
            def _(copy=copy):
                copy.wait_send()
    small_wait(out_ref, dbs, dbr)
    small_wait(sbuf, ss, sr)
    total = jnp.sum(sbuf[...], axis=0) * (1.0 / (nb * sub))
    picked = total[:comps, 0:n_col]
    for row in range(1, n_row):
        picked = jnp.where(z == row, total[:comps, row * n_col:(row + 1) * n_col], picked)
    stress_ref[...] = picked


def fused_local(n_row, probes, ham_blocks, strain_blocks, block_cols, odd_coeffs):
    n_col = 4
    nb = n_row * n_col
    probe_count, block = probes.shape
    _, groups, cap, comps = strain_blocks.shape[:4]
    slots = groups * cap
    sub = probe_count // nb
    chunks = 3
    bf16, f32 = jnp.bfloat16, jnp.float32
    dma = pltpu.SemaphoreType.DMA
    vmem = pl.BlockSpec(memory_space=pltpu.VMEM)
    hbm = pl.BlockSpec(memory_space=pltpu.HBM)
    density, stress = pl.pallas_call(
        functools.partial(fused_kernel, n_row),
        out_shape=(
            jax.ShapeDtypeStruct((nb, sub, block), bf16),
            jax.ShapeDtypeStruct((comps, n_col), f32),
        ),
        in_specs=[hbm] * 5,
        out_specs=(vmem, vmem),
        scratch_shapes=[
            pltpu.VMEM((nb, groups, cap, block, block), bf16),
            pltpu.VMEM((nb, probe_count, block), bf16),
            pltpu.VMEM((nb, sub, block), bf16),
            pltpu.VMEM((nb, cap, groups), jnp.int32),
            pltpu.SMEM((nb, cap, groups), jnp.int32),
            pltpu.SMEM((2,), f32),
            pltpu.VMEM((nb, 8, 128), f32),
            pltpu.VMEM((slots, comps, block, block), bf16),
            pltpu.VMEM((nb, block, sub), bf16),
            pltpu.VMEM((nb, block, sub), bf16),
            pltpu.VMEM((nb, block, sub), bf16),
            pltpu.VMEM((nb, sub, block), bf16),
            pltpu.VMEM((nb, sub, block), bf16),
            dma((nb, chunks, 4)), dma((nb, chunks)),
            dma((nb, 4)), dma((nb,)),
            dma((nb,)), dma((nb,)),
            dma((nb,)), dma((nb,)),
            dma((nb,)), dma((nb,)),
            dma((nb,)), dma((nb,)),
            dma((nb,)), dma((nb,)),
            dma((7,)),
        ],
        compiler_params=pltpu.CompilerParams(
            collective_id=0, has_side_effects=True, vmem_limit_bytes=40 * 1024 * 1024
        ),
    )(
        probes,
        ham_blocks.reshape(groups, cap, block, block),
        strain_blocks.reshape(slots, comps, block, block),
        block_cols.reshape(groups, cap).T,
        odd_coeffs,
    )
    return density.reshape(probe_count, block), stress


def along_row(panel):
    return lax.all_gather(panel, "col", axis=1, tiled=True)


def along_col(panel):
    return lax.all_gather(panel, "row", axis=1, tiled=True)


def down_sum(partial_value):
    return lax.psum_scatter(
        partial_value.astype(jnp.bfloat16), "row", scatter_dimension=1, tiled=True
    ).astype(jnp.float32)


def local(probes, ham_blocks, strain_blocks, block_cols, odd_coeffs):
    probe_count = probes.shape[0]
    block_size = ham_blocks.shape[-1]
    own_rows = probes.shape[1] // block_size
    components = strain_blocks.shape[3]
    ham_local, strain_local, cols_local = (
        lax.all_to_all(ham_blocks, "col", split_axis=1, concat_axis=0, tiled=True),
        lax.all_to_all(strain_blocks, "col", split_axis=1, concat_axis=0, tiled=True),
        lax.all_to_all(block_cols, "col", split_axis=1, concat_axis=0, tiled=True),
    )
    grid_rows = ham_local.shape[0]
    slot_cap = ham_local.shape[2]
    slot_count = grid_rows * slot_cap
    ham_slots = ham_local.reshape(slot_count, block_size, block_size)
    col_slots = cols_local.reshape(slot_count)
    group_width = lax.axis_size("row") * own_rows
    local_cols = col_slots - lax.axis_index("col") * group_width
    filled = col_slots >= 0
    safe_cols = jnp.clip(local_cols, 0, group_width - 1).astype(jnp.int32)
    placement = (
        (safe_cols[:, None] == jnp.arange(group_width, dtype=jnp.int32)[None, :]) & filled[:, None]
    ).astype(jnp.float32)

    def backward(gathered):
        spread = jnp.repeat(gathered.reshape(probe_count, grid_rows, block_size), slot_cap, axis=1)
        contrib = jnp.einsum("psa,sab->psb", spread, ham_slots, preferred_element_type=jnp.float32)
        placed = jnp.einsum("psb,sj->pjb", contrib, placement, precision=lax.Precision.HIGHEST)
        return placed.reshape(probe_count, group_width * block_size)

    probes_row = along_row(probes)
    first_term = down_sum(backward(probes_row)).astype(jnp.bfloat16)
    first_col = along_col(first_term)
    picked = jnp.take(first_col.reshape(probe_count, group_width, block_size), safe_cols, axis=1)
    contrib = jnp.einsum("psb,sab->psa", picked, ham_slots, preferred_element_type=jnp.float32)
    summed = contrib.reshape(probe_count, grid_rows, slot_cap, block_size).sum(axis=2)
    partial_two = summed.reshape(probe_count, grid_rows * block_size)
    row_piece = lax.psum_scatter(
        partial_two.astype(jnp.bfloat16), "col", scatter_dimension=1, tiled=True
    ).astype(jnp.float32)
    second_term = (2.0 * row_piece - probes.astype(jnp.float32)).astype(jnp.bfloat16)
    second_row = along_row(second_term)
    third_term = 2.0 * down_sum(backward(second_row)) - first_term.astype(jnp.float32)
    density = (odd_coeffs[0] * first_term.astype(jnp.float32) + odd_coeffs[1] * third_term).astype(
        jnp.bfloat16
    )
    density_col = along_col(density)
    own_probes = jnp.repeat(
        probes_row.reshape(probe_count, grid_rows, block_size), slot_cap, axis=1
    )
    others = jnp.take(density_col.reshape(probe_count, group_width, block_size), safe_cols, axis=1)
    pair_tiles = jnp.einsum(
        "psa,psb->sab", own_probes, others, preferred_element_type=jnp.float32
    ).astype(jnp.bfloat16)
    strain_slots = strain_local.reshape(slot_count, components, block_size, block_size)
    slot_terms = jnp.einsum(
        "skab,sab->ks", strain_slots, pair_tiles, preferred_element_type=jnp.float32
    )
    row_terms = slot_terms.reshape(components, grid_rows, slot_cap).sum(axis=2) / probe_count
    stress = lax.psum(row_terms, "col")
    return (density, stress)


def solution(mesh):
    placed = (
        P("groups", ("row", "col")),
        P(("groups", "row", "col"), None, None, None, None),
        P(("groups", "row", "col"), None, None, None, None, None),
        P(("groups", "row", "col"), None, None),
        P(),
    )
    n_row, n_col = mesh.shape["row"], mesh.shape["col"]

    def pick(*args):
        probes, ham_blocks = args[0], args[1]
        one_block = probes.shape[1] == ham_blocks.shape[-1] and ham_blocks.shape[0] == 1
        held = n_row * n_col * (2 * ham_blocks.size + 2 * probes.size)
        whole_rows = probes.shape[0] % (16 * n_row * n_col) == 0
        if n_row == 4 and n_col == 4 and one_block and whole_rows and held <= 16 * 1024 * 1024:
            return fused_local(n_row, *args)
        return local(*args)

    return jax.shard_map(
        pick,
        mesh=mesh,
        in_specs=placed,
        out_specs=(P("groups", ("col", "row")), P("groups", "row")),
        check_vma=False,
    )
```

```python
import functools

import jax
import jax.numpy as jnp
from jax import lax
from jax.experimental import pallas as pl
from jax.experimental.pallas import tpu as pltpu
from jax.sharding import PartitionSpec as P

MESH = pl.DeviceIdType.MESH


def fused_kernel(
    n_row,
    probes_ref, ham_ref, strain_ref, cols_ref, coeffs_ref,
    out_ref, stress_ref,
    hbuf, mbuf, pbuf, xbuf, cbuf, csm, coeffs, sbuf, strain_buf, x0t, x1t, x2t, dsend, dmine,
    hs, hr, ps, pr, xs, xr, cs, cr, das, dar, dbs, dbr, ss, sr, loc,
):
    n_col = 4
    nb = n_row * n_col
    grp = lax.axis_index("groups")
    z = lax.axis_index("row")
    c = lax.axis_index("col")
    me = z * n_col + c
    sib = c + 1 - 2 * (c % 2)
    yc = (c + 2) % 4
    ysib = sib + 2 - 4 * (sib // 2)
    groups, cap = hbuf.shape[1:3]
    slots = groups * cap
    chunks = hr.shape[1]
    sub = xbuf.shape[1]
    comps = strain_buf.shape[1]

    def dev(row, col):
        return (grp, row, col)

    barrier = pltpu.get_barrier_semaphore()

    def greet(d, carry):
        k = (me + d) % nb
        pl.semaphore_signal(barrier, inc=1, device_id=dev(k // n_col, k % n_col), device_id_type=MESH)
        return carry

    lax.fori_loop(1, nb, greet, 0)
    own = pl.ds(pl.multiple_of(me * sub, sub), sub)
    local_copies = [
        pltpu.make_async_copy(src, dst, loc.at[n])
        for n, (src, dst) in enumerate(
            [
                (cols_ref, cbuf.at[me]),
                (probes_ref.at[own], xbuf.at[me]),
                (coeffs_ref, coeffs),
                (ham_ref, hbuf.at[me]),
                (probes_ref, pbuf.at[me]),
                (strain_ref, strain_buf),
            ]
        )
    ]
    for copy in local_copies:
        copy.start()
    pl.semaphore_wait(barrier, nb - 1)

    waits = []

    def remote(src, dst, send, recv, target):
        return pltpu.make_async_remote_copy(
            src_ref=src, dst_ref=dst, send_sem=send, recv_sem=recv, device_id=target, device_id_type=MESH
        )

    def launch(copy, pred=None):
        if pred is None:
            copy.start()
        else:
            @pl.when(pred)
            def _():
                copy.start()
        waits.append((copy, pred))

    sent_small = []

    def small(src_of, dst, send, recv):
        def copy_to(d):
            k = (me + d) % nb
            return remote(src_of(k), dst, send.at[d], recv.at[me], dev(k // n_col, k % n_col))

        def go(t, carry):
            copy_to((t + nb // 2) % nb).start()
            return carry

        lax.fori_loop(0, nb // 2, go, 0)

        def rest(t, carry):
            copy_to(t).start()
            return carry

        lax.fori_loop(1, nb // 2, rest, 0)
        sent_small.append(copy_to)

    def small_wait(dst, send, recv):
        def arrived(d, carry):
            k = (me + d) % nb
            remote(dst.at[k], dst.at[k], send.at[d], recv.at[k], dev(z, sib)).wait_recv()
            return carry

        lax.fori_loop(1, nb, arrived, 0)

    small(lambda k: cols_ref, cbuf.at[me], cs, cr)
    small(lambda k: probes_ref.at[pl.ds(pl.multiple_of(k * sub, sub), sub)], xbuf.at[me], xs, xr)

    def sends_third(row):
        return jnp.logical_or(row == 0, row == n_row - 1)

    def ham_piece(org, m):
        return hbuf.at[org, (org // n_col + m) % groups]

    def with_third(org, m, pred):
        if m < 2:
            return pred
        third = sends_third(org // n_col)
        return third if pred is None else jnp.logical_and(pred, third)

    def ham_send(org, m, way, target, pred=None):
        src = ham_ref.at[(z + m) % groups] if org is me else ham_piece(org, m)
        launch(
            remote(src, ham_piece(org, m), hs.at[org, m, way], hr.at[org, m], target),
            with_third(org, m, pred),
        )

    def ham_recv(org, m):
        copy = remote(ham_piece(org, m), ham_piece(org, m), hs.at[org, m, 0], hr.at[org, m], dev(z, sib))
        if m < 2:
            copy.wait_recv()
        else:
            @pl.when(sends_third(org // n_col))
            def _():
                copy.wait_recv()

    def probe_send(org, m, way, target, pred=None):
        src = probes_ref if org is me else pbuf.at[org]
        launch(remote(src, pbuf.at[org], ps.at[org, way], pr.at[org], target), pred)

    def probe_recv(org, m):
        remote(pbuf.at[org], pbuf.at[org], ps.at[org, 0], pr.at[org], dev(z, sib)).wait_recv()

    up, down = z + 1, z - 1
    has_up, has_down = z < n_row - 1, z > 0

    def first(send, pieces):
        for m in range(pieces):
            send(me, m, 0, dev(jnp.minimum(up, n_row - 1), c), has_up)
            send(me, m, 1, dev(jnp.maximum(down, 0), c), has_down)
            send(me, m, 2, dev(z, yc))
            send(me, m, 3, dev(z, sib))

    def wave(d, send, recv, pieces):
        for m in range(pieces):
            if d < n_row:
                for sgn in (-1, 1):
                    zo = z + sgn * d
                    ok = zo >= 0 if sgn < 0 else zo <= n_row - 1
                    org = jnp.clip(zo, 0, n_row - 1) * n_col + c

                    @pl.when(ok)
                    def _():
                        recv(org, m)
                    if d < n_row - 1:
                        if sgn < 0:
                            send(org, m, 0, dev(jnp.minimum(up, n_row - 1), c), jnp.logical_and(ok, has_up))
                        else:
                            send(org, m, 1, dev(jnp.maximum(down, 0), c), jnp.logical_and(ok, has_down))
                    send(org, m, 2, dev(z, yc), ok)
                    send(org, m, 3, dev(z, sib), ok)
            for sgn in (-1, 1) if d > 1 else (1,):
                zo = z + sgn * (d - 1)
                ok = zo >= 0 if sgn < 0 else zo <= n_row - 1
                org = jnp.clip(zo, 0, n_row - 1) * n_col + yc

                @pl.when(ok)
                def _():
                    recv(org, m)
                send(org, m, 3, dev(z, sib), ok)

    def last(recv, pieces):
        for row in range(n_row):
            for m in range(pieces):
                recv(row * n_col + sib, m)
                recv(row * n_col + ysib, m)

    first(ham_send, chunks)
    first(probe_send, 1)

    small_wait(cbuf, cs, cr)
    local_copies[0].wait()
    cols_copy = pltpu.make_async_copy(cbuf, csm, loc.at[6])
    cols_copy.start()
    small_wait(xbuf, xs, xr)
    local_copies[1].wait()

    def turn(j, carry):
        x0t[j] = xbuf[j].astype(jnp.float32).T.astype(jnp.bfloat16)
        return carry

    lax.fori_loop(0, nb, turn, 0, unroll=4)
    cols_copy.wait()
    local_copies[2].wait()

    for d in range(1, n_row + 1):
        wave(d, ham_send, ham_recv, chunks)
    local_copies[3].wait()
    last(ham_recv, chunks)
    wave(1, probe_send, probe_recv, 1)

    def col_of(i, s):
        return jnp.clip(csm[i, s % cap, s // cap], 0, nb - 1)

    def mirrored(a, g):
        way = (a - g) % n_row
        return way == 1 or (way == 2 and g in (0, n_row - 1))

    def mirror(a, g):
        def one_row(w, carry):
            i = a * n_col + w
            for s in range(cap):
                raw = csm[i, s, g]
                j = jnp.clip(raw, 0, nb - 1)
                place = jnp.int32(0)
                for t in range(1, cap):
                    place = jnp.where(csm[j, t, a] == i, t, place)
                block = hbuf[j, a, place].T
                mbuf[i, g, s] = jnp.where(raw >= 0, block, jnp.zeros_like(block))
            return carry

        lax.fori_loop(0, n_col, one_row, 0, unroll=True)

        def put_back(w, carry):
            hbuf[a * n_col + w, g] = mbuf[a * n_col + w, g]
            return carry

        return lambda: lax.fori_loop(0, n_col, put_back, 0)

    def product(x_ref, i):
        weights = jnp.concatenate([x_ref[col_of(i, s)] for s in range(slots)], axis=0)
        rows = jnp.concatenate([hbuf[i, s // cap, s % cap] for s in range(slots)], axis=1)
        return jnp.dot(rows, weights, preferred_element_type=jnp.float32)

    def each_row(body):
        def step(i, carry):
            body(i)
            return carry

        lax.fori_loop(0, nb, step, 0, unroll=4)

    def one(i):
        x1t[i] = product(x0t, i).astype(jnp.bfloat16)

    def two(i):
        x2t[i] = (2.0 * product(x1t, i) - x0t[i].astype(jnp.float32)).astype(jnp.bfloat16)

    mine_out = c * n_row + z

    def to_pair(k):
        return k != me, remote(
            dsend.at[k], dmine.at[me], das.at[k], dar.at[me], dev(k // n_col, k % n_col)
        )

    def to_out(k):
        return k != mine_out, remote(
            dsend.at[k], out_ref.at[me], dbs.at[k], dbr.at[me], dev(k % n_row, k // n_row)
        )

    def three(i):
        prior = x1t[i].astype(jnp.float32)
        third = 2.0 * product(x2t, i) - prior
        dense = coeffs[0] * prior + coeffs[1] * third
        dsend[i] = dense.T.astype(jnp.bfloat16)

    backs = [mirror(a, g) for a in range(n_row) for g in range(groups) if mirrored(a, g)]
    for back in backs:
        back()
    each_row(one)
    wave(2, probe_send, probe_recv, 1)
    each_row(two)
    wave(3, probe_send, probe_recv, 1)
    each_row(three)

    def start_pair(t, carry):
        row = (z + 2 + t // n_col) % n_row
        pred, copy = to_pair(row * n_col + (c + t) % n_col)
        pl.when(pred)(copy.start)
        return carry

    def start_out(k, carry):
        pred, copy = to_out(k)
        pl.when(pred)(copy.start)
        return carry

    lax.fori_loop(0, nb, start_pair, 0)
    lax.fori_loop(0, nb, start_out, 0)
    dmine[me] = dsend[me]
    out_ref[me] = dsend[mine_out]
    for d in range(4, n_row + 1):
        wave(d, probe_send, probe_recv, 1)
    last(probe_recv, 1)

    small_wait(dmine, das, dar)
    local_copies[4].wait()
    local_copies[5].wait()
    dens = dmine[...].reshape(nb * sub, dmine.shape[2])
    dens_t = dens.astype(jnp.float32).T.astype(jnp.bfloat16)
    lane = lax.broadcasted_iota(jnp.int32, (comps, 128), 1)

    def pair(s, part):
        col = col_of(me, s)
        tile = jnp.dot(dens_t, pbuf[col], preferred_element_type=jnp.float32)
        sums = jnp.concatenate(
            [
                jnp.sum(strain_buf[s, k].astype(jnp.float32) * tile, axis=0, keepdims=True)
                for k in range(comps)
            ],
            axis=0,
        )
        return part + jnp.where(lane == col, jnp.sum(sums, axis=1, keepdims=True), 0.0)

    part = lax.fori_loop(0, slots, pair, jnp.zeros((comps, 128), jnp.float32), unroll=2)
    sbuf[me] = jnp.concatenate([part, jnp.zeros((sbuf.shape[1] - comps, 128), jnp.float32)], axis=0)
    small(lambda k: sbuf.at[me], sbuf.at[me], ss, sr)
    def sent(k, carry):
        for pred, copy in (to_pair(k), to_out(k)):
            pl.when(pred)(copy.wait_send)
        return carry

    lax.fori_loop(0, nb, sent, 0)

    def sent_others(d, carry):
        for copy_to in sent_small:
            copy_to(d).wait_send()
        return carry

    lax.fori_loop(1, nb, sent_others, 0)
    for copy, pred in waits:
        if pred is None:
            copy.wait_send()
        else:
            @pl.when(pred)
            def _(copy=copy):
                copy.wait_send()
    small_wait(out_ref, dbs, dbr)
    small_wait(sbuf, ss, sr)
    total = jnp.sum(sbuf[...], axis=0) * (1.0 / (nb * sub))
    picked = total[:comps, 0:n_col]
    for row in range(1, n_row):
        picked = jnp.where(z == row, total[:comps, row * n_col:(row + 1) * n_col], picked)
    stress_ref[...] = picked


def fused_local(n_row, probes, ham_blocks, strain_blocks, block_cols, odd_coeffs):
    n_col = 4
    nb = n_row * n_col
    probe_count, block = probes.shape
    _, groups, cap, comps = strain_blocks.shape[:4]
    slots = groups * cap
    sub = probe_count // nb
    chunks = 3
    bf16, f32 = jnp.bfloat16, jnp.float32
    dma = pltpu.SemaphoreType.DMA
    vmem = pl.BlockSpec(memory_space=pltpu.VMEM)
    hbm = pl.BlockSpec(memory_space=pltpu.HBM)
    density, stress = pl.pallas_call(
        functools.partial(fused_kernel, n_row),
        out_shape=(
            jax.ShapeDtypeStruct((nb, sub, block), bf16),
            jax.ShapeDtypeStruct((comps, n_col), f32),
        ),
        in_specs=[hbm] * 5,
        out_specs=(vmem, vmem),
        scratch_shapes=[
            pltpu.VMEM((nb, groups, cap, block, block), bf16),
            pltpu.VMEM((nb, groups, cap, block, block), bf16),
            pltpu.VMEM((nb, probe_count, block), bf16),
            pltpu.VMEM((nb, sub, block), bf16),
            pltpu.VMEM((nb, cap, groups), jnp.int32),
            pltpu.SMEM((nb, cap, groups), jnp.int32),
            pltpu.SMEM((2,), f32),
            pltpu.VMEM((nb, 8, 128), f32),
            pltpu.VMEM((slots, comps, block, block), bf16),
            pltpu.VMEM((nb, block, sub), bf16),
            pltpu.VMEM((nb, block, sub), bf16),
            pltpu.VMEM((nb, block, sub), bf16),
            pltpu.VMEM((nb, sub, block), bf16),
            pltpu.VMEM((nb, sub, block), bf16),
            dma((nb, chunks, 4)), dma((nb, chunks)),
            dma((nb, 4)), dma((nb,)),
            dma((nb,)), dma((nb,)),
            dma((nb,)), dma((nb,)),
            dma((nb,)), dma((nb,)),
            dma((nb,)), dma((nb,)),
            dma((nb,)), dma((nb,)),
            dma((7,)),
        ],
        compiler_params=pltpu.CompilerParams(
            collective_id=0, has_side_effects=True, vmem_limit_bytes=64 * 1024 * 1024 - 65536
        ),
    )(
        probes,
        ham_blocks.reshape(groups, cap, block, block),
        strain_blocks.reshape(slots, comps, block, block),
        block_cols.reshape(groups, cap).T,
        odd_coeffs,
    )
    return density.reshape(probe_count, block), stress


def along_row(panel):
    return lax.all_gather(panel, "col", axis=1, tiled=True)


def along_col(panel):
    return lax.all_gather(panel, "row", axis=1, tiled=True)


def down_sum(partial_value):
    return lax.psum_scatter(
        partial_value.astype(jnp.bfloat16), "row", scatter_dimension=1, tiled=True
    ).astype(jnp.float32)


def local(probes, ham_blocks, strain_blocks, block_cols, odd_coeffs):
    probe_count = probes.shape[0]
    block_size = ham_blocks.shape[-1]
    own_rows = probes.shape[1] // block_size
    components = strain_blocks.shape[3]
    ham_local, strain_local, cols_local = (
        lax.all_to_all(ham_blocks, "col", split_axis=1, concat_axis=0, tiled=True),
        lax.all_to_all(strain_blocks, "col", split_axis=1, concat_axis=0, tiled=True),
        lax.all_to_all(block_cols, "col", split_axis=1, concat_axis=0, tiled=True),
    )
    grid_rows = ham_local.shape[0]
    slot_cap = ham_local.shape[2]
    slot_count = grid_rows * slot_cap
    ham_slots = ham_local.reshape(slot_count, block_size, block_size)
    col_slots = cols_local.reshape(slot_count)
    group_width = lax.axis_size("row") * own_rows
    local_cols = col_slots - lax.axis_index("col") * group_width
    filled = col_slots >= 0
    safe_cols = jnp.clip(local_cols, 0, group_width - 1).astype(jnp.int32)
    placement = (
        (safe_cols[:, None] == jnp.arange(group_width, dtype=jnp.int32)[None, :]) & filled[:, None]
    ).astype(jnp.float32)

    def backward(gathered):
        spread = jnp.repeat(gathered.reshape(probe_count, grid_rows, block_size), slot_cap, axis=1)
        contrib = jnp.einsum("psa,sab->psb", spread, ham_slots, preferred_element_type=jnp.float32)
        placed = jnp.einsum("psb,sj->pjb", contrib, placement, precision=lax.Precision.HIGHEST)
        return placed.reshape(probe_count, group_width * block_size)

    probes_row = along_row(probes)
    first_term = down_sum(backward(probes_row)).astype(jnp.bfloat16)
    first_col = along_col(first_term)
    picked = jnp.take(first_col.reshape(probe_count, group_width, block_size), safe_cols, axis=1)
    contrib = jnp.einsum("psb,sab->psa", picked, ham_slots, preferred_element_type=jnp.float32)
    summed = contrib.reshape(probe_count, grid_rows, slot_cap, block_size).sum(axis=2)
    partial_two = summed.reshape(probe_count, grid_rows * block_size)
    row_piece = lax.psum_scatter(
        partial_two.astype(jnp.bfloat16), "col", scatter_dimension=1, tiled=True
    ).astype(jnp.float32)
    second_term = (2.0 * row_piece - probes.astype(jnp.float32)).astype(jnp.bfloat16)
    second_row = along_row(second_term)
    third_term = 2.0 * down_sum(backward(second_row)) - first_term.astype(jnp.float32)
    density = (odd_coeffs[0] * first_term.astype(jnp.float32) + odd_coeffs[1] * third_term).astype(
        jnp.bfloat16
    )
    density_col = along_col(density)
    own_probes = jnp.repeat(
        probes_row.reshape(probe_count, grid_rows, block_size), slot_cap, axis=1
    )
    others = jnp.take(density_col.reshape(probe_count, group_width, block_size), safe_cols, axis=1)
    pair_tiles = jnp.einsum(
        "psa,psb->sab", own_probes, others, preferred_element_type=jnp.float32
    ).astype(jnp.bfloat16)
    strain_slots = strain_local.reshape(slot_count, components, block_size, block_size)
    slot_terms = jnp.einsum(
        "skab,sab->ks", strain_slots, pair_tiles, preferred_element_type=jnp.float32
    )
    row_terms = slot_terms.reshape(components, grid_rows, slot_cap).sum(axis=2) / probe_count
    stress = lax.psum(row_terms, "col")
    return (density, stress)


def solution(mesh):
    placed = (
        P("groups", ("row", "col")),
        P(("groups", "row", "col"), None, None, None, None),
        P(("groups", "row", "col"), None, None, None, None, None),
        P(("groups", "row", "col"), None, None),
        P(),
    )
    n_row, n_col = mesh.shape["row"], mesh.shape["col"]

    def pick(*args):
        probes, ham_blocks = args[0], args[1]
        one_block = probes.shape[1] == ham_blocks.shape[-1] and ham_blocks.shape[0] == 1
        held = n_row * n_col * (2 * ham_blocks.size + 2 * probes.size)
        whole_rows = probes.shape[0] % (16 * n_row * n_col) == 0
        if n_row == 4 and n_col == 4 and one_block and whole_rows and held <= 16 * 1024 * 1024:
            return fused_local(n_row, *args)
        return local(*args)

    return jax.shard_map(
        pick,
        mesh=mesh,
        in_specs=placed,
        out_specs=(P("groups", ("col", "row")), P("groups", "row")),
        check_vma=False,
    )
```

```python
import functools

import jax
import jax.numpy as jnp
from jax import lax
from jax.experimental import pallas as pl
from jax.experimental.pallas import tpu as pltpu
from jax.sharding import PartitionSpec as P

MESH = pl.DeviceIdType.MESH


def fused_kernel(
    n_row,
    probes_ref, ham_ref, strain_ref, cols_ref, coeffs_ref,
    out_ref, stress_ref,
    hbuf, mbuf, pbuf, xbuf, cbuf, csm, coeffs, sbuf, strain_buf, x0t, x1t, x2t, dsend, dmine,
    hs, hr, ps, pr, xs, xr, cs, cr, das, dar, dbs, dbr, ss, sr, loc,
):
    n_col = 4
    nb = n_row * n_col
    grp = lax.axis_index("groups")
    z = lax.axis_index("row")
    c = lax.axis_index("col")
    me = z * n_col + c
    sib = c + 1 - 2 * (c % 2)
    yc = (c + 2) % 4
    ysib = sib + 2 - 4 * (sib // 2)
    groups, cap = hbuf.shape[1:3]
    slots = groups * cap
    chunks = hr.shape[1]
    sub = xbuf.shape[1]
    comps = strain_buf.shape[1]

    def dev(row, col):
        return (grp, row, col)

    barrier = pltpu.get_barrier_semaphore()

    def greet(d, carry):
        k = (me + d) % nb
        pl.semaphore_signal(barrier, inc=1, device_id=dev(k // n_col, k % n_col), device_id_type=MESH)
        return carry

    lax.fori_loop(1, nb, greet, 0)
    own = pl.ds(pl.multiple_of(me * sub, sub), sub)
    local_copies = [
        pltpu.make_async_copy(src, dst, loc.at[n])
        for n, (src, dst) in enumerate(
            [
                (cols_ref, cbuf.at[me]),
                (probes_ref.at[own], xbuf.at[me]),
                (coeffs_ref, coeffs),
                (ham_ref, hbuf.at[me]),
                (probes_ref, pbuf.at[me]),
                (strain_ref, strain_buf),
            ]
        )
    ]
    for copy in local_copies:
        copy.start()
    pl.semaphore_wait(barrier, nb - 1)

    waits = []

    def remote(src, dst, send, recv, target):
        return pltpu.make_async_remote_copy(
            src_ref=src, dst_ref=dst, send_sem=send, recv_sem=recv, device_id=target, device_id_type=MESH
        )

    def launch(copy, pred=None):
        if pred is None:
            copy.start()
        else:
            @pl.when(pred)
            def _():
                copy.start()
        waits.append((copy, pred))

    sent_small = []

    def small(src_of, dst, send, recv):
        def copy_to(d):
            k = (me + d) % nb
            return remote(src_of(k), dst, send.at[d], recv.at[me], dev(k // n_col, k % n_col))

        def go(t, carry):
            copy_to((t + nb // 2) % nb).start()
            return carry

        lax.fori_loop(0, nb // 2, go, 0)

        def rest(t, carry):
            copy_to(t).start()
            return carry

        lax.fori_loop(1, nb // 2, rest, 0)
        sent_small.append(copy_to)

    def small_wait(dst, send, recv):
        def arrived(d, carry):
            k = (me + d) % nb
            remote(dst.at[k], dst.at[k], send.at[d], recv.at[k], dev(z, sib)).wait_recv()
            return carry

        lax.fori_loop(1, nb, arrived, 0)

    small(lambda k: cols_ref, cbuf.at[me], cs, cr)
    small(lambda k: probes_ref.at[pl.ds(pl.multiple_of(k * sub, sub), sub)], xbuf.at[me], xs, xr)

    def sends_third(row):
        return jnp.logical_or(row == 0, row == n_row - 1)

    def ham_piece(org, m):
        return hbuf.at[org, (org // n_col + m) % groups]

    def with_third(org, m, pred):
        if m < 2:
            return pred
        third = sends_third(org // n_col)
        return third if pred is None else jnp.logical_and(pred, third)

    def ham_send(org, m, way, target, pred=None):
        src = ham_ref.at[(z + m) % groups] if org is me else ham_piece(org, m)
        launch(
            remote(src, ham_piece(org, m), hs.at[org, m, way], hr.at[org, m], target),
            with_third(org, m, pred),
        )

    def ham_recv(org, m):
        copy = remote(ham_piece(org, m), ham_piece(org, m), hs.at[org, m, 0], hr.at[org, m], dev(z, sib))
        if m < 2:
            copy.wait_recv()
        else:
            @pl.when(sends_third(org // n_col))
            def _():
                copy.wait_recv()

    half = probes_ref.shape[0] // 2

    def probe_part(ref, m):
        return ref.at[pl.ds(m * half, half)]

    def probe_send(org, m, way, target, pred=None):
        src = probe_part(probes_ref if org is me else pbuf.at[org], m)
        launch(remote(src, probe_part(pbuf.at[org], m), ps.at[org, m, way], pr.at[org, m], target), pred)

    def probe_recv(org, m):
        part = probe_part(pbuf.at[org], m)
        remote(part, part, ps.at[org, m, 0], pr.at[org, m], dev(z, sib)).wait_recv()

    up, down = z + 1, z - 1
    has_up, has_down = z < n_row - 1, z > 0

    def first(send, pieces):
        for m in range(pieces):
            send(me, m, 0, dev(jnp.minimum(up, n_row - 1), c), has_up)
            send(me, m, 1, dev(jnp.maximum(down, 0), c), has_down)
            send(me, m, 2, dev(z, yc))
            send(me, m, 3, dev(z, sib))

    def wave(d, send, recv, pieces):
        for m in range(pieces):
            if d < n_row:
                for sgn in (-1, 1):
                    zo = z + sgn * d
                    ok = zo >= 0 if sgn < 0 else zo <= n_row - 1
                    org = jnp.clip(zo, 0, n_row - 1) * n_col + c

                    @pl.when(ok)
                    def _():
                        recv(org, m)
                    if d < n_row - 1:
                        if sgn < 0:
                            send(org, m, 0, dev(jnp.minimum(up, n_row - 1), c), jnp.logical_and(ok, has_up))
                        else:
                            send(org, m, 1, dev(jnp.maximum(down, 0), c), jnp.logical_and(ok, has_down))
                    send(org, m, 2, dev(z, yc), ok)
                    send(org, m, 3, dev(z, sib), ok)
            for sgn in (-1, 1) if d > 1 else (1,):
                zo = z + sgn * (d - 1)
                ok = zo >= 0 if sgn < 0 else zo <= n_row - 1
                org = jnp.clip(zo, 0, n_row - 1) * n_col + yc

                @pl.when(ok)
                def _():
                    recv(org, m)
                send(org, m, 3, dev(z, sib), ok)

    def last(recv, pieces):
        for row in range(n_row):
            for m in range(pieces):
                recv(row * n_col + sib, m)
                recv(row * n_col + ysib, m)

    def chain(d):
        for col in (c, yc):
            for sgn in (-1, 1) if (d - (col is yc)) > 0 else (1,):
                step = d - 1 if col is yc else d
                if step > n_row - 1:
                    continue
                zo = z + sgn * step
                ok = zo >= 0 if sgn < 0 else zo <= n_row - 1
                org = jnp.clip(zo, 0, n_row - 1) * n_col + col

                @pl.when(ok)
                def _():
                    probe_recv(org, 1)
                if step < n_row - 1 and (sgn < 0 or step == 0):
                    probe_send(org, 1, 0, dev(jnp.minimum(up, n_row - 1), c), jnp.logical_and(ok, has_up))
                if step < n_row - 1 and (sgn > 0 or step == 0):
                    probe_send(org, 1, 1, dev(jnp.maximum(down, 0), c), jnp.logical_and(ok, has_down))
                probe_send(org, 1, 3, dev(z, sib), ok)

    first(ham_send, chunks)
    first(probe_send, 2)

    small_wait(cbuf, cs, cr)
    local_copies[0].wait()
    cols_copy = pltpu.make_async_copy(cbuf, csm, loc.at[6])
    cols_copy.start()
    small_wait(xbuf, xs, xr)
    local_copies[1].wait()

    def turn(j, carry):
        x0t[j] = xbuf[j].astype(jnp.float32).T.astype(jnp.bfloat16)
        return carry

    lax.fori_loop(0, nb, turn, 0, unroll=4)
    cols_copy.wait()
    local_copies[2].wait()

    for d in range(1, n_row + 1):
        wave(d, ham_send, ham_recv, chunks)
    local_copies[3].wait()
    last(ham_recv, chunks)
    wave(1, probe_send, probe_recv, 1)
    chain(1)

    def col_of(i, s):
        return jnp.clip(csm[i, s % cap, s // cap], 0, nb - 1)

    def mirrored(a, g):
        way = (a - g) % n_row
        return way == 1 or (way == 2 and g in (0, n_row - 1))

    def mirror(a, g):
        def one_row(w, carry):
            i = a * n_col + w
            for s in range(cap):
                raw = csm[i, s, g]
                j = jnp.clip(raw, 0, nb - 1)
                place = jnp.int32(0)
                for t in range(1, cap):
                    place = jnp.where(csm[j, t, a] == i, t, place)
                block = hbuf[j, a, place].T
                mbuf[i, g, s] = jnp.where(raw >= 0, block, jnp.zeros_like(block))
            return carry

        lax.fori_loop(0, n_col, one_row, 0, unroll=True)

        def put_back(w, carry):
            hbuf[a * n_col + w, g] = mbuf[a * n_col + w, g]
            return carry

        return lambda: lax.fori_loop(0, n_col, put_back, 0)

    def product(x_ref, i):
        weights = jnp.concatenate([x_ref[col_of(i, s)] for s in range(slots)], axis=0)
        rows = jnp.concatenate([hbuf[i, s // cap, s % cap] for s in range(slots)], axis=1)
        return jnp.dot(rows, weights, preferred_element_type=jnp.float32)

    def each_row(body):
        def step(i, carry):
            body(i)
            return carry

        lax.fori_loop(0, nb, step, 0, unroll=4)

    def one(i):
        x1t[i] = product(x0t, i).astype(jnp.bfloat16)

    def two(i):
        x2t[i] = (2.0 * product(x1t, i) - x0t[i].astype(jnp.float32)).astype(jnp.bfloat16)

    mine_out = c * n_row + z

    def to_pair(k):
        return k != me, remote(
            dsend.at[k], dmine.at[me], das.at[k], dar.at[me], dev(k // n_col, k % n_col)
        )

    def to_out(k):
        return k != mine_out, remote(
            dsend.at[k], out_ref.at[me], dbs.at[k], dbr.at[me], dev(k % n_row, k // n_row)
        )

    def three(i):
        prior = x1t[i].astype(jnp.float32)
        third = 2.0 * product(x2t, i) - prior
        dense = coeffs[0] * prior + coeffs[1] * third
        dsend[i] = dense.T.astype(jnp.bfloat16)

    backs = [mirror(a, g) for a in range(n_row) for g in range(groups) if mirrored(a, g)]
    for back in backs:
        back()
    each_row(one)
    wave(2, probe_send, probe_recv, 1)
    chain(2)
    each_row(two)
    wave(3, probe_send, probe_recv, 1)
    chain(3)
    each_row(three)

    def start_pair(t, carry):
        row = (z + 2 + t // n_col) % n_row
        pred, copy = to_pair(row * n_col + (c + t) % n_col)
        pl.when(pred)(copy.start)
        return carry

    def start_out(k, carry):
        pred, copy = to_out(k)
        pl.when(pred)(copy.start)
        return carry

    lax.fori_loop(0, nb, start_pair, 0)
    lax.fori_loop(0, nb, start_out, 0)
    dmine[me] = dsend[me]
    out_ref[me] = dsend[mine_out]
    for d in range(4, n_row + 1):
        wave(d, probe_send, probe_recv, 1)
        chain(d)
    last(probe_recv, 2)

    small_wait(dmine, das, dar)
    local_copies[4].wait()
    local_copies[5].wait()
    dens = dmine[...].reshape(nb * sub, dmine.shape[2])
    dens_t = dens.astype(jnp.float32).T.astype(jnp.bfloat16)
    lane = lax.broadcasted_iota(jnp.int32, (comps, 128), 1)

    def pair(s, part):
        col = col_of(me, s)
        tile = jnp.dot(dens_t, pbuf[col], preferred_element_type=jnp.float32)
        sums = jnp.concatenate(
            [
                jnp.sum(strain_buf[s, k].astype(jnp.float32) * tile, axis=0, keepdims=True)
                for k in range(comps)
            ],
            axis=0,
        )
        return part + jnp.where(lane == col, jnp.sum(sums, axis=1, keepdims=True), 0.0)

    part = lax.fori_loop(0, slots, pair, jnp.zeros((comps, 128), jnp.float32), unroll=2)
    sbuf[me] = jnp.concatenate([part, jnp.zeros((sbuf.shape[1] - comps, 128), jnp.float32)], axis=0)
    small(lambda k: sbuf.at[me], sbuf.at[me], ss, sr)
    def sent(k, carry):
        for pred, copy in (to_pair(k), to_out(k)):
            pl.when(pred)(copy.wait_send)
        return carry

    lax.fori_loop(0, nb, sent, 0)

    def sent_others(d, carry):
        for copy_to in sent_small:
            copy_to(d).wait_send()
        return carry

    lax.fori_loop(1, nb, sent_others, 0)
    for copy, pred in waits:
        if pred is None:
            copy.wait_send()
        else:
            @pl.when(pred)
            def _(copy=copy):
                copy.wait_send()
    small_wait(out_ref, dbs, dbr)
    small_wait(sbuf, ss, sr)
    total = jnp.sum(sbuf[...], axis=0) * (1.0 / (nb * sub))
    picked = total[:comps, 0:n_col]
    for row in range(1, n_row):
        picked = jnp.where(z == row, total[:comps, row * n_col:(row + 1) * n_col], picked)
    stress_ref[...] = picked


def fused_local(n_row, probes, ham_blocks, strain_blocks, block_cols, odd_coeffs):
    n_col = 4
    nb = n_row * n_col
    probe_count, block = probes.shape
    _, groups, cap, comps = strain_blocks.shape[:4]
    slots = groups * cap
    sub = probe_count // nb
    chunks = 3
    bf16, f32 = jnp.bfloat16, jnp.float32
    dma = pltpu.SemaphoreType.DMA
    vmem = pl.BlockSpec(memory_space=pltpu.VMEM)
    hbm = pl.BlockSpec(memory_space=pltpu.HBM)
    density, stress = pl.pallas_call(
        functools.partial(fused_kernel, n_row),
        out_shape=(
            jax.ShapeDtypeStruct((nb, sub, block), bf16),
            jax.ShapeDtypeStruct((comps, n_col), f32),
        ),
        in_specs=[hbm] * 5,
        out_specs=(vmem, vmem),
        scratch_shapes=[
            pltpu.VMEM((nb, groups, cap, block, block), bf16),
            pltpu.VMEM((nb, groups, cap, block, block), bf16),
            pltpu.VMEM((nb, probe_count, block), bf16),
            pltpu.VMEM((nb, sub, block), bf16),
            pltpu.VMEM((nb, cap, groups), jnp.int32),
            pltpu.SMEM((nb, cap, groups), jnp.int32),
            pltpu.SMEM((2,), f32),
            pltpu.VMEM((nb, 8, 128), f32),
            pltpu.VMEM((slots, comps, block, block), bf16),
            pltpu.VMEM((nb, block, sub), bf16),
            pltpu.VMEM((nb, block, sub), bf16),
            pltpu.VMEM((nb, block, sub), bf16),
            pltpu.VMEM((nb, sub, block), bf16),
            pltpu.VMEM((nb, sub, block), bf16),
            dma((nb, chunks, 4)), dma((nb, chunks)),
            dma((nb, 2, 4)), dma((nb, 2)),
            dma((nb,)), dma((nb,)),
            dma((nb,)), dma((nb,)),
            dma((nb,)), dma((nb,)),
            dma((nb,)), dma((nb,)),
            dma((nb,)), dma((nb,)),
            dma((7,)),
        ],
        compiler_params=pltpu.CompilerParams(
            collective_id=0, has_side_effects=True, vmem_limit_bytes=64 * 1024 * 1024 - 65536
        ),
    )(
        probes,
        ham_blocks.reshape(groups, cap, block, block),
        strain_blocks.reshape(slots, comps, block, block),
        block_cols.reshape(groups, cap).T,
        odd_coeffs,
    )
    return density.reshape(probe_count, block), stress


def along_row(panel):
    return lax.all_gather(panel, "col", axis=1, tiled=True)


def along_col(panel):
    return lax.all_gather(panel, "row", axis=1, tiled=True)


def down_sum(partial_value):
    return lax.psum_scatter(
        partial_value.astype(jnp.bfloat16), "row", scatter_dimension=1, tiled=True
    ).astype(jnp.float32)


def local(probes, ham_blocks, strain_blocks, block_cols, odd_coeffs):
    probe_count = probes.shape[0]
    block_size = ham_blocks.shape[-1]
    own_rows = probes.shape[1] // block_size
    components = strain_blocks.shape[3]
    ham_local, strain_local, cols_local = (
        lax.all_to_all(ham_blocks, "col", split_axis=1, concat_axis=0, tiled=True),
        lax.all_to_all(strain_blocks, "col", split_axis=1, concat_axis=0, tiled=True),
        lax.all_to_all(block_cols, "col", split_axis=1, concat_axis=0, tiled=True),
    )
    grid_rows = ham_local.shape[0]
    slot_cap = ham_local.shape[2]
    slot_count = grid_rows * slot_cap
    ham_slots = ham_local.reshape(slot_count, block_size, block_size)
    col_slots = cols_local.reshape(slot_count)
    group_width = lax.axis_size("row") * own_rows
    local_cols = col_slots - lax.axis_index("col") * group_width
    filled = col_slots >= 0
    safe_cols = jnp.clip(local_cols, 0, group_width - 1).astype(jnp.int32)
    placement = (
        (safe_cols[:, None] == jnp.arange(group_width, dtype=jnp.int32)[None, :]) & filled[:, None]
    ).astype(jnp.float32)

    def backward(gathered):
        spread = jnp.repeat(gathered.reshape(probe_count, grid_rows, block_size), slot_cap, axis=1)
        contrib = jnp.einsum("psa,sab->psb", spread, ham_slots, preferred_element_type=jnp.float32)
        placed = jnp.einsum("psb,sj->pjb", contrib, placement, precision=lax.Precision.HIGHEST)
        return placed.reshape(probe_count, group_width * block_size)

    probes_row = along_row(probes)
    first_term = down_sum(backward(probes_row)).astype(jnp.bfloat16)
    first_col = along_col(first_term)
    picked = jnp.take(first_col.reshape(probe_count, group_width, block_size), safe_cols, axis=1)
    contrib = jnp.einsum("psb,sab->psa", picked, ham_slots, preferred_element_type=jnp.float32)
    summed = contrib.reshape(probe_count, grid_rows, slot_cap, block_size).sum(axis=2)
    partial_two = summed.reshape(probe_count, grid_rows * block_size)
    row_piece = lax.psum_scatter(
        partial_two.astype(jnp.bfloat16), "col", scatter_dimension=1, tiled=True
    ).astype(jnp.float32)
    second_term = (2.0 * row_piece - probes.astype(jnp.float32)).astype(jnp.bfloat16)
    second_row = along_row(second_term)
    third_term = 2.0 * down_sum(backward(second_row)) - first_term.astype(jnp.float32)
    density = (odd_coeffs[0] * first_term.astype(jnp.float32) + odd_coeffs[1] * third_term).astype(
        jnp.bfloat16
    )
    density_col = along_col(density)
    own_probes = jnp.repeat(
        probes_row.reshape(probe_count, grid_rows, block_size), slot_cap, axis=1
    )
    others = jnp.take(density_col.reshape(probe_count, group_width, block_size), safe_cols, axis=1)
    pair_tiles = jnp.einsum(
        "psa,psb->sab", own_probes, others, preferred_element_type=jnp.float32
    ).astype(jnp.bfloat16)
    strain_slots = strain_local.reshape(slot_count, components, block_size, block_size)
    slot_terms = jnp.einsum(
        "skab,sab->ks", strain_slots, pair_tiles, preferred_element_type=jnp.float32
    )
    row_terms = slot_terms.reshape(components, grid_rows, slot_cap).sum(axis=2) / probe_count
    stress = lax.psum(row_terms, "col")
    return (density, stress)


def solution(mesh):
    placed = (
        P("groups", ("row", "col")),
        P(("groups", "row", "col"), None, None, None, None),
        P(("groups", "row", "col"), None, None, None, None, None),
        P(("groups", "row", "col"), None, None),
        P(),
    )
    n_row, n_col = mesh.shape["row"], mesh.shape["col"]

    def pick(*args):
        probes, ham_blocks = args[0], args[1]
        one_block = probes.shape[1] == ham_blocks.shape[-1] and ham_blocks.shape[0] == 1
        held = n_row * n_col * (2 * ham_blocks.size + 2 * probes.size)
        whole_rows = probes.shape[0] % (16 * n_row * n_col) == 0
        if n_row == 4 and n_col == 4 and one_block and whole_rows and held <= 16 * 1024 * 1024:
            return fused_local(n_row, *args)
        return local(*args)

    return jax.shard_map(
        pick,
        mesh=mesh,
        in_specs=placed,
        out_specs=(P("groups", ("col", "row")), P("groups", "row")),
        check_vma=False,
    )
```
